32 devices in a mesh: tp: 4 (over x, core), ha: 2 (over y), wa: 4 (over z).
Axes of the slice: x: 2, y: 2, z: 4, core: 2. Of those that a mesh axis runs over, the one named last changes fastest.
Arguments:
- queries: bfloat16 [1, 4, 8, 128, 3072], P(None, 'ha', 'wa', None, 'tp'), may hold values from -128 to 128
- keys: bfloat16 [1, 4, 8, 128, 3072], P(None, 'ha', 'wa', None, 'tp'), may hold values from -4.5 to 4.5
- values: bfloat16 [1, 4, 8, 128, 3072], P(None, 'ha', 'wa', None, 'tp'), may hold values from -6 to 6
- grad_out: bfloat16 [1, 4, 8, 128, 3072], P(None, 'ha', 'wa', None, 'tp'), may hold values from -6 to 6
- out_proj: bfloat16 [3072, 3072], P(('ha', 'wa'), 'tp'), may hold values from -0.109375 to 0.109375
Outputs:
- grad_queries: bfloat16 [1, 4, 8, 128, 3072], P(None, 'ha', 'wa', None, 'tp')
- grad_keys: bfloat16 [1, 4, 8, 128, 3072], P(None, 'ha', 'wa', None, 'tp')
- grad_values: bfloat16 [1, 4, 8, 128, 3072], P(None, 'ha', 'wa', None, 'tp')
The draws below stay inside these ranges and needn't reach their ends.
All inputs are finite; a program needn't handle non-finite values.
Results may differ from the reference program's by a relative error of at most 0.014.
Values may be sent and summed in bfloat16 or wider, within the bound.
A program may use at most 128 MiB of HBM per device.

```python
import jax
import jax.numpy as jnp
from jax import lax

D = 3072
HEADS = 24
HEAD = 128
TILE = 128
TF = 1
HD = 3072
NTH = 4
NTW = 8


def shared_keys(key):
    base = jax.random.normal(jax.random.fold_in(key, 7), (TF, NTH, NTW, TILE, HEADS * HEAD), jnp.float32)
    base = jnp.clip(base, -4.0, 4.0)
    return base


def draw_keys(key, part):
    return shared_keys(key).astype(jnp.bfloat16)


def draw_queries(key, part):
    base = jax.random.normal(jax.random.fold_in(key, 11), (TF, NTH, NTW, TILE, HEADS * HEAD), jnp.float32)
    base = jnp.clip(base, -4.0, 4.0)
    return base.astype(jnp.bfloat16)


def block_levels(own_key, shape, shards, low, largest):
    gain, own = 1.0, jax.random.fold_in(own_key, 6)
    for dim, shards_of in shards:
        draws = jnp.exp(jax.random.uniform(jax.random.fold_in(own, dim), (shards_of,), jnp.float32, low / len(shards), largest / len(shards)))
        gain = gain * jnp.repeat(draws, shape[dim] // shards_of).reshape([-1 if axis == dim else 1 for axis in range(len(shape))])
    return gain


def centred(rng, dims, deviation, most, cuts=(), kind=jnp.bfloat16):
    entries = deviation * jax.random.normal(rng, dims, jnp.float32)
    if cuts:
        entries = entries * block_levels(rng, dims, cuts, -0.22, 0.18)
    return jnp.clip(entries, -most, most).astype(kind)


def setup_inputs(seed: int = 0) -> dict:
    seeds = jax.random.split(jax.random.key(seed), 6)
    return {
        "queries": draw_queries(jax.random.fold_in(seeds[5], 71), 0),
        "keys": draw_keys(jax.random.fold_in(seeds[5], 71), 0),
        "values": centred(seeds[2], (TF, NTH, NTW, TILE, HD), 1.0, 6.0, ((1, 2), (2, 4), (4, 4))),
        "grad_out": centred(seeds[3], (TF, NTH, NTW, TILE, D), 1.0, 6.0, ((1, 2), (2, 4), (4, 4))),
        "out_proj": centred(seeds[4], (D, HD), D ** -0.5, 0.109375, ((0, 8), (1, 4))),
    }


def tile_backward(query_blk, key_blk, value_blk, grad_blk, softmax_scale):
    f32 = jnp.float32
    scores = jnp.einsum('qtd,qld->qtl', query_blk.astype(f32), key_blk.astype(f32)) * softmax_scale
    scores = scores - jnp.max(scores, axis=-1, keepdims=True)
    expo = jnp.exp(scores)
    probs = expo / jnp.sum(expo, axis=-1, keepdims=True)
    probs_lo = probs.astype(jnp.bfloat16)
    attn = jnp.einsum('qtl,qld->qtd', probs_lo.astype(f32), value_blk.astype(f32))
    delta = jnp.sum(grad_blk.astype(f32) * attn, axis=-1, keepdims=True)
    grad_probs = jnp.einsum('qtd,qld->qtl', grad_blk.astype(f32), value_blk.astype(f32))
    grad_scores = (probs * (grad_probs - delta) * softmax_scale).astype(jnp.bfloat16)
    grad_query = jnp.einsum('qtl,qld->qtd', grad_scores.astype(f32), key_blk.astype(f32))
    grad_key = jnp.einsum('qtl,qtd->qld', grad_scores.astype(f32), query_blk.astype(f32))
    grad_value = jnp.einsum('qtl,qtd->qld', probs_lo.astype(f32), grad_blk.astype(f32))
    return grad_query, grad_key, grad_value


def reference(queries, keys, values, grad_out, out_proj):
    frames, tile_rows, tile_cols, tile_len, features = queries.shape
    head_count = features // HEAD
    flat_rows = grad_out.reshape(-1, grad_out.shape[-1])
    grad_attn = jnp.dot(flat_rows, out_proj, preferred_element_type=jnp.float32).astype(jnp.bfloat16)
    grad_attn = grad_attn.reshape(queries.shape)
    span = min(3, frames)
    grid_f, grid_r, grid_c = jnp.meshgrid(jnp.arange(frames, dtype=jnp.int32), jnp.arange(tile_rows, dtype=jnp.int32), jnp.arange(tile_cols, dtype=jnp.int32), indexing='ij')
    start_f = jnp.clip(grid_f.reshape(-1) - 1, 0, frames - span).astype(jnp.int32)
    start_r = jnp.clip(grid_r.reshape(-1) - 1, 0, tile_rows - 3).astype(jnp.int32)
    start_c = jnp.clip(grid_c.reshape(-1) - 1, 0, tile_cols - 3).astype(jnp.int32)
    tile_count = start_f.shape[0]
    zero_idx = jnp.zeros((), jnp.int32)
    softmax_scale = HEAD ** -0.5

    def split_heads(array):
        return jnp.moveaxis(array.reshape(frames, tile_rows, tile_cols, tile_len, head_count, HEAD), 4, 0)

    def join_heads(array):
        return jnp.moveaxis(array, 0, 4).reshape(frames, tile_rows, tile_cols, tile_len, features)

    def one_head(operands):
        query_h, key_h, value_h, grad_h = operands
        both = jnp.stack([key_h, value_h])

        def take(first, second, third):
            return lax.dynamic_slice(both, (zero_idx, first, second, third, zero_idx, zero_idx), (2, span, 3, 3, tile_len, HEAD))

        window = jax.vmap(take)(start_f, start_r, start_c)
        key_blk = window[:, 0].reshape(tile_count, -1, HEAD)
        value_blk = window[:, 1].reshape(tile_count, -1, HEAD)
        query_blk = query_h.reshape(tile_count, tile_len, HEAD)
        grad_blk = grad_h.reshape(tile_count, tile_len, HEAD)
        grad_query, grad_key, grad_value = tile_backward(query_blk, key_blk, value_blk, grad_blk, softmax_scale)
        pieces = jnp.stack([grad_key, grad_value], 1).reshape(tile_count, 2, span, 3, 3, tile_len, HEAD)
        totals = jnp.zeros((2, frames, tile_rows, tile_cols, tile_len, HEAD), jnp.float32)

        def add_one(index, totals):
            start = (zero_idx, start_f[index], start_r[index], start_c[index], zero_idx, zero_idx)
            current = lax.dynamic_slice(totals, start, (2, span, 3, 3, tile_len, HEAD))
            return lax.dynamic_update_slice(totals, current + pieces[index], start)

        totals = lax.fori_loop(0, tile_count, add_one, totals)
        grad_query = grad_query.reshape(frames, tile_rows, tile_cols, tile_len, HEAD).astype(jnp.bfloat16)
        return grad_query, totals[0].astype(jnp.bfloat16), totals[1].astype(jnp.bfloat16)

    grad_q, grad_k, grad_v = lax.map(one_head, (split_heads(queries), split_heads(keys), split_heads(values), split_heads(grad_attn)))
    return (join_heads(grad_q), join_heads(grad_k), join_heads(grad_v))
```

```python
import functools

import jax
import jax.numpy as jnp
from jax import lax
from jax.experimental import pallas as pl
from jax.experimental.pallas import tpu as pltpu
from jax.sharding import PartitionSpec as P

HEAD = 128
MESH = pl.DeviceIdType.MESH
AROUND = ((0, -1), (0, 1), (-1, 0), (1, 0), (-1, -1), (-1, 1), (1, -1), (1, 1))
NT = (((1,), (1,)), ((), ()))
TN = (((0,), (0,)), ((), ()))


def inner_part(step, count):
    return {0: (1, count), -1: (1, 1), 1: (count, 1)}[step]


def outer_part(step, count):
    return {0: (1, count), -1: (0, 1), 1: (count + 1, 1)}[step]


def kernel(
    sizes,
    q_ref,
    k_ref,
    v_ref,
    g_ref,
    w_ref,
    dq_ref,
    dk_ref,
    dv_ref,
    k_ext,
    v_ext,
    g_all,
    w_all,
    ga,
    probs,
    totals,
    own,
    out_halo,
    *rest,
):
    in_halo = rest[:8]
    (
        local_sem,
        g_send,
        g_recv,
        kv_send,
        kv_recv,
        z_send,
        z_recv,
        y_send,
        y_recv,
        h_send,
        h_recv,
    ) = rest[8:]
    tp_n, ha_n, wa_n = sizes
    tp, ha, wa = (lax.axis_index(a) for a in ("tp", "ha", "wa"))
    rows, cols, tile, feat = k_ref.shape
    heads = feat // HEAD
    depth = w_ref.shape[0]
    f32, bf16 = jnp.float32, jnp.bfloat16

    def exists(step_r, step_c):
        r, c = ha + step_r, wa + step_c
        return (r >= 0) & (r < ha_n) & (c >= 0) & (c < wa_n)

    def at(step_r, step_c):
        return {"tp": tp, "ha": ha + step_r, "wa": wa + step_c}

    barrier = pltpu.get_barrier_semaphore()
    for k in range(1, tp_n):
        pl.semaphore_signal(
            barrier, inc=1, device_id={"tp": lax.rem(tp + k, tp_n), "ha": ha, "wa": wa}, device_id_type=MESH
        )
    for k in range(1, ha_n):
        pl.semaphore_signal(
            barrier, inc=1, device_id={"tp": tp, "ha": lax.rem(ha + k, ha_n), "wa": wa}, device_id_type=MESH
        )
    greeted = jnp.int32(tp_n - 1 + ha_n - 1)
    for step_r, step_c in AROUND:
        if step_c == 0:
            continue
        here = exists(step_r, step_c)
        greeted = greeted + here.astype(jnp.int32)

        @pl.when(here)
        def _():
            pl.semaphore_signal(barrier, inc=1, device_id=at(step_r, step_c), device_id_type=MESH)

    k_own = pltpu.make_async_copy(k_ref, k_ext.at[pl.ds(1, rows), pl.ds(1, cols)], local_sem.at[0])
    v_own = pltpu.make_async_copy(v_ref, v_ext.at[pl.ds(1, rows), pl.ds(1, cols)], local_sem.at[1])
    g_own = pltpu.make_async_copy(g_ref, g_all.at[tp], local_sem.at[2])
    w_rows = lambda block: pl.ds(pl.multiple_of(block * depth, 16), depth)
    w_own = pltpu.make_async_copy(w_ref, w_all.at[w_rows(ha * wa_n + wa)], local_sem.at[3])
    for copy in (k_own, v_own, g_own, w_own):
        copy.start()
    pl.semaphore_wait(barrier, greeted)

    def kv_copy(which, n):
        step_r, step_c = AROUND[n]
        src_r, len_r = inner_part(step_r, rows)
        src_c, len_c = inner_part(step_c, cols)
        dst_r, _ = outer_part(-step_r, rows)
        dst_c, _ = outer_part(-step_c, cols)
        src, dst = ((k_ref, k_ext), (v_ref, v_ext))[which]
        return pltpu.make_async_remote_copy(
            src_ref=src.at[pl.ds(src_r - 1, len_r), pl.ds(src_c - 1, len_c)],
            dst_ref=dst.at[pl.ds(dst_r, len_r), pl.ds(dst_c, len_c)],
            send_sem=kv_send.at[which, n],
            recv_sem=kv_recv.at[which, n],
            device_id=at(step_r, step_c),
            device_id_type=MESH,
        )

    def kv_arrival(which, n):
        step_r, step_c = AROUND[n]
        dst_r, len_r = outer_part(-step_r, rows)
        dst_c, len_c = outer_part(-step_c, cols)
        dst = (k_ext, v_ext)[which].at[pl.ds(dst_r, len_r), pl.ds(dst_c, len_c)]
        return pltpu.make_async_remote_copy(
            src_ref=dst,
            dst_ref=dst,
            send_sem=kv_send.at[which, n],
            recv_sem=kv_recv.at[which, n],
            device_id=at(-step_r, -step_c),
            device_id_type=MESH,
        )

    def each_way(do, sign=1):
        for n, (step_r, step_c) in enumerate(AROUND):

            @pl.when(exists(sign * step_r, sign * step_c))
            def _():
                do(n)

    each_way(lambda n: kv_copy(0, n).start())

    def g_copy(k):
        return pltpu.make_async_remote_copy(
            src_ref=g_ref,
            dst_ref=g_all.at[tp],
            send_sem=g_send.at[k - 1],
            recv_sem=g_recv.at[k - 1],
            device_id={"tp": lax.rem(tp + k, tp_n), "ha": ha, "wa": wa},
            device_id_type=MESH,
        )

    for k in range(1, tp_n):
        g_copy(k).start()

    def z_copy(way, step, source):
        where = w_all.at[w_rows(ha * wa_n + source)]
        return pltpu.make_async_remote_copy(
            src_ref=where,
            dst_ref=where,
            send_sem=z_send.at[way, step],
            recv_sem=z_recv.at[way, step],
            device_id={"tp": tp, "ha": ha, "wa": wa + (1, -1)[way]},
            device_id_type=MESH,
        )

    def y_copy(j, source, k, row):
        where = w_all.at[w_rows(row * wa_n + source)]
        return pltpu.make_async_remote_copy(
            src_ref=where,
            dst_ref=where,
            send_sem=y_send.at[j, k - 1],
            recv_sem=y_recv.at[j, k - 1],
            device_id={"tp": tp, "ha": lax.rem(ha + k, ha_n), "wa": wa},
            device_id_type=MESH,
        )

    def next_exists(way):
        return (wa + 1 < wa_n) if way == 0 else (wa >= 1)

    def source_of(way, step):
        source = wa - 1 - step if way == 0 else wa + 1 + step
        return source, ((source >= 0) if way == 0 else (source < wa_n))

    w_own.wait()
    for way in range(2):

        @pl.when(next_exists(way))
        def _():
            z_copy(way, 0, wa).start()

    for k in range(1, ha_n):
        y_copy(0, wa, k, ha).start()
    each_way(lambda n: kv_copy(1, n).start())

    def pass_on(step):
        for way in range(2):
            source, there = source_of(way, step)

            @pl.when(there)
            def _():
                z_copy(way, step, source).wait_recv()
                if step + 1 < wa_n - 1:

                    @pl.when(next_exists(way))
                    def _():
                        z_copy(way, step + 1, source).start()

                for k in range(1, ha_n):
                    y_copy(1 + way * (wa_n - 1) + step, source, k, ha).start()

    row_base, col_base = ha * rows, wa * cols
    scale = HEAD**-0.5

    def place(t):
        r, c = t // cols, t % cols
        start_r = jnp.clip(row_base + r - 1, 0, rows * ha_n - 3) - row_base + 1
        start_c = jnp.clip(col_base + c - 1, 0, cols * wa_n - 3) - col_base + 1
        return r, c, start_r, start_c

    def lanes(head):
        return pl.ds(pl.multiple_of(head * HEAD, HEAD), HEAD)

    def window(ext, start_r, start_c, head):
        return ext[pl.ds(start_r, 3), pl.ds(start_c, 3), :, lanes(head)].reshape(9 * tile, HEAD)

    def softmax_heads(first, last):
        @pl.loop(first, last)
        def _(head):
            for t in range(rows * cols):
                r, c, start_r, start_c = place(t)
                query = q_ref[r, c, :, lanes(head)]
                scores = lax.dot_general(
                    window(k_ext, start_r, start_c, head), query, NT, preferred_element_type=f32
                )
                scores = scores * scale
                expo = jnp.exp(scores - jnp.max(scores, axis=0, keepdims=True))
                inverse = 1.0 / jnp.sum(expo, axis=0, keepdims=True)
                probs[head, t] = (expo * inverse).astype(bf16)

    k_own.wait()
    each_way(lambda n: kv_arrival(0, n).wait_recv(), sign=-1)
    chunks = wa_n - 1
    for i in range(chunks):
        softmax_heads(i * heads // chunks, (i + 1) * heads // chunks)
        pass_on(i)

    g_own.wait()
    for k in range(1, tp_n):
        g_copy(k).wait_recv()
    v_own.wait()
    each_way(lambda n: kv_arrival(1, n).wait_recv(), sign=-1)
    for k in range(1, ha_n):
        row = lax.rem(ha + ha_n - k, ha_n)
        y_copy(0, wa, k, row).wait_recv()
        for way in range(2):
            for step in range(wa_n - 1):
                source, there = source_of(way, step)

                @pl.when(there)
                def _():
                    y_copy(1 + way * (wa_n - 1) + step, source, k, row).wait_recv()

    block = 256 if feat % 256 == 0 else 128

    @pl.loop(0, feat // block)
    def _(i):
        columns = pl.ds(pl.multiple_of(i * block, block), block)
        for half in range(2):
            m = rows * cols * tile // 2
            total = jnp.zeros((m, block), f32)
            for p in range(tp_n):
                total = total + jnp.dot(
                    g_all[p, half * m : (half + 1) * m, :],
                    w_all[p * feat : (p + 1) * feat, columns],
                    preferred_element_type=f32,
                )
            ga[half * m : (half + 1) * m, columns] = total.astype(bf16)

    def halo_copy(head, n):
        step_r, step_c = AROUND[n]
        src_r, len_r = outer_part(step_r, rows)
        src_c, len_c = outer_part(step_c, cols)
        return pltpu.make_async_remote_copy(
            src_ref=out_halo.at[head, :, pl.ds(src_r, len_r), pl.ds(src_c, len_c)],
            dst_ref=in_halo[n].at[head],
            send_sem=h_send.at[head, n],
            recv_sem=h_recv.at[head, n],
            device_id=at(step_r, step_c),
            device_id_type=MESH,
        )

    @pl.loop(0, heads)
    def _(head):
        totals[...] = jnp.zeros_like(totals)
        for t in range(rows * cols):
            r, c, start_r, start_c = place(t)
            grad = ga[t * tile : (t + 1) * tile, lanes(head)]
            prob = probs[head, t]
            grad_probs = lax.dot_general(
                window(v_ext, start_r, start_c, head), grad, NT, preferred_element_type=f32
            )
            weighted = prob.astype(f32) * grad_probs
            delta = jnp.sum(weighted, axis=0, keepdims=True)
            grad_scores = ((weighted - prob.astype(f32) * delta) * scale).astype(bf16)
            query = q_ref[r, c, :, lanes(head)]
            keys = window(k_ext, start_r, start_c, head)
            dq_ref[r, c, :, lanes(head)] = lax.dot_general(
                grad_scores, keys, TN, preferred_element_type=f32
            ).astype(bf16)
            shape = (3, 3, tile, HEAD)
            part = (pl.ds(start_r, 3), pl.ds(start_c, 3))
            grad_keys = jnp.dot(grad_scores, query, preferred_element_type=f32)
            totals[0, *part] += grad_keys.reshape(shape)
            grad_values = jnp.dot(prob, grad, preferred_element_type=f32)
            totals[1, *part] += grad_values.reshape(shape)
        own[head] = totals[:, 1 : rows + 1, 1 : cols + 1]
        out_halo[head] = totals[...].astype(bf16)
        each_way(lambda n: halo_copy(head, n).start())

    @pl.loop(0, heads)
    def _(head):
        for n, (step_r, step_c) in enumerate(AROUND):

            @pl.when(exists(-step_r, -step_c))
            def _():
                halo_copy(head, n).wait_recv()
                to_r, len_r = inner_part(-step_r, rows)
                to_c, len_c = inner_part(-step_c, cols)
                own[head, :, to_r - 1 : to_r - 1 + len_r, to_c - 1 : to_c - 1 + len_c] += in_halo[n][
                    head
                ].astype(f32)

        dk_ref[:, :, :, lanes(head)] = own[head, 0].astype(bf16)
        dv_ref[:, :, :, lanes(head)] = own[head, 1].astype(bf16)

    for which in range(2):
        each_way(lambda n: kv_copy(which, n).wait_send())
    for k in range(1, tp_n):
        g_copy(k).wait_send()
    for way in range(2):

        @pl.when(next_exists(way))
        def _():
            z_copy(way, 0, wa).wait_send()

        for step in range(wa_n - 1):
            source, there = source_of(way, step)

            if step + 1 < wa_n - 1:

                @pl.when(there & next_exists(way))
                def _():
                    z_copy(way, step + 1, source).wait_send()

            @pl.when(there)
            def _():
                for k in range(1, ha_n):
                    y_copy(1 + way * (wa_n - 1) + step, source, k, ha).wait_send()

    for k in range(1, ha_n):
        y_copy(0, wa, k, ha).wait_send()

    @pl.loop(0, heads)
    def _(head):
        each_way(lambda n: halo_copy(head, n).wait_send())


def local(queries, keys, values, grad_out, out_proj):
    frames, rows, cols, tile, feat = queries.shape
    heads = feat // HEAD
    tokens = rows * cols * tile
    tp_n, ha_n, wa_n = sizes = tuple(lax.axis_size(a) for a in ("tp", "ha", "wa"))
    blocks = queries.shape[1:]
    bf16, f32 = jnp.bfloat16, jnp.float32
    vmem, dma = pltpu.VMEM, pltpu.SemaphoreType.DMA
    length = lambda step, count: count if step == 0 else 1
    in_halo = [
        vmem((heads, 2, length(r, rows), length(c, cols), tile, HEAD), bf16) for r, c in AROUND
    ]
    whole = pl.BlockSpec(memory_space=pltpu.VMEM)
    anywhere = pl.BlockSpec(memory_space=pl.ANY)
    hops = wa_n - 1
    outs = pl.pallas_call(
        functools.partial(kernel, sizes),
        out_shape=[jax.ShapeDtypeStruct(blocks, bf16)] * 3,
        in_specs=[whole, anywhere, anywhere, anywhere, anywhere],
        out_specs=[whole] * 3,
        scratch_shapes=[
            vmem((rows + 2, cols + 2, tile, feat), bf16),
            vmem((rows + 2, cols + 2, tile, feat), bf16),
            vmem((tp_n, tokens, feat), bf16),
            vmem((out_proj.shape[0] * ha_n * wa_n, feat), bf16),
            vmem((tokens, feat), bf16),
            vmem((heads, rows * cols, 9 * tile, tile), bf16),
            vmem((2, rows + 2, cols + 2, tile, HEAD), f32),
            vmem((heads, 2, rows, cols, tile, HEAD), f32),
            vmem((heads, 2, rows + 2, cols + 2, tile, HEAD), bf16),
            *in_halo,
            dma((4,)),
            dma((tp_n - 1,)),
            dma((tp_n - 1,)),
            dma((2, 8)),
            dma((2, 8)),
            dma((2, hops)),
            dma((2, hops)),
            dma((1 + 2 * hops, ha_n - 1)),
            dma((1 + 2 * hops, ha_n - 1)),
            dma((heads, 8)),
            dma((heads, 8)),
        ],
        compiler_params=pltpu.CompilerParams(
            collective_id=0, has_side_effects=True, vmem_limit_bytes=60 * 2**20
        ),
    )(
        queries.reshape(blocks),
        keys.reshape(blocks),
        values.reshape(blocks),
        grad_out.reshape(tokens, feat),
        out_proj,
    )
    return tuple(out.reshape(queries.shape) for out in outs)


def solution(mesh):
    tiles = P(None, "ha", "wa", None, "tp")
    return jax.shard_map(
        local,
        mesh=mesh,
        in_specs=(tiles, tiles, tiles, tiles, P(("ha", "wa"), "tp")),
        out_specs=(tiles,) * 3,
        check_vma=False,
    )
```

```python
import functools

import jax
import jax.numpy as jnp
from jax import lax
from jax.experimental import pallas as pl
from jax.experimental.pallas import tpu as pltpu
from jax.sharding import PartitionSpec as P

HEAD = 128
MESH = pl.DeviceIdType.MESH
AROUND = ((0, -1), (0, 1), (-1, 0), (1, 0), (-1, -1), (-1, 1), (1, -1), (1, 1))
COLUMNS, ROWS, CORNERS = (0, 1), (2, 3), (4, 5, 6, 7)
NT = (((1,), (1,)), ((), ()))
TN = (((0,), (0,)), ((), ()))


def inner_part(step, count):
    return {0: (1, count), -1: (1, 1), 1: (count, 1)}[step]


def outer_part(step, count):
    return {0: (1, count), -1: (0, 1), 1: (count + 1, 1)}[step]


def kernel(
    sizes,
    q_ref,
    k_ref,
    v_ref,
    g_ref,
    w_ref,
    dq_ref,
    dk_ref,
    dv_ref,
    k_ext,
    v_ext,
    g_all,
    w_all,
    ga,
    probs,
    totals,
    own,
    out_halo,
    *rest,
):
    in_halo = rest[:8]
    (
        local_sem,
        g_send,
        g_recv,
        kv_send,
        kv_recv,
        z_send,
        z_recv,
        y_send,
        y_recv,
        h_send,
        h_recv,
    ) = rest[8:]
    tp_n, ha_n, wa_n = sizes
    tp, ha, wa = (lax.axis_index(a) for a in ("tp", "ha", "wa"))
    rows, cols, tile, feat = k_ref.shape
    heads = feat // HEAD
    depth = w_ref.shape[0]
    f32, bf16 = jnp.float32, jnp.bfloat16

    def exists(step_r, step_c):
        r, c = ha + step_r, wa + step_c
        return (r >= 0) & (r < ha_n) & (c >= 0) & (c < wa_n)

    def at(step_r, step_c):
        return {"tp": tp, "ha": ha + step_r, "wa": wa + step_c}

    barrier = pltpu.get_barrier_semaphore()
    for k in range(1, tp_n):
        pl.semaphore_signal(
            barrier, inc=1, device_id={"tp": lax.rem(tp + k, tp_n), "ha": ha, "wa": wa}, device_id_type=MESH
        )
    for k in range(1, ha_n):
        pl.semaphore_signal(
            barrier, inc=1, device_id={"tp": tp, "ha": lax.rem(ha + k, ha_n), "wa": wa}, device_id_type=MESH
        )
    greeted = jnp.int32(tp_n - 1 + ha_n - 1)
    for n in COLUMNS:
        step_r, step_c = AROUND[n]
        here = exists(step_r, step_c)
        greeted = greeted + here.astype(jnp.int32)

        @pl.when(here)
        def _():
            pl.semaphore_signal(barrier, inc=1, device_id=at(step_r, step_c), device_id_type=MESH)

    k_own = pltpu.make_async_copy(k_ref, k_ext.at[pl.ds(1, rows), pl.ds(1, cols)], local_sem.at[0])
    v_own = pltpu.make_async_copy(v_ref, v_ext.at[pl.ds(1, rows), pl.ds(1, cols)], local_sem.at[1])
    g_own = pltpu.make_async_copy(g_ref, g_all.at[tp], local_sem.at[2])
    w_rows = lambda block: pl.ds(pl.multiple_of(block * depth, 16), depth)
    w_own = pltpu.make_async_copy(w_ref, w_all.at[w_rows(ha * wa_n + wa)], local_sem.at[3])
    for copy in (k_own, v_own, g_own, w_own):
        copy.start()
    pl.semaphore_wait(barrier, greeted)

    def kv_copy(which, n):
        step_r, step_c = AROUND[n]
        src_c, len_c = inner_part(step_c, cols)
        dst_c, _ = outer_part(-step_c, cols)
        src, dst = ((k_ref, k_ext), (v_ref, v_ext))[which]
        if step_r and step_c:
            src_r, len_r = outer_part(step_r, rows)
            dst_r = src_r
            there = at(0, step_c)
            src = dst.at[pl.ds(src_r, len_r), pl.ds(src_c, len_c)]
        else:
            src_r, len_r = inner_part(step_r, rows)
            dst_r, _ = outer_part(-step_r, rows)
            there = at(step_r, step_c)
            src = src.at[pl.ds(src_r - 1, len_r), pl.ds(src_c - 1, len_c)]
        return pltpu.make_async_remote_copy(
            src_ref=src,
            dst_ref=dst.at[pl.ds(dst_r, len_r), pl.ds(dst_c, len_c)],
            send_sem=kv_send.at[which, n],
            recv_sem=kv_recv.at[which, n],
            device_id=there,
            device_id_type=MESH,
        )

    def kv_arrival(which, n):
        step_r, step_c = AROUND[n]
        dst_r, len_r = outer_part(step_r if step_c else -step_r, rows)
        dst_c, len_c = outer_part(-step_c, cols)
        dst = (k_ext, v_ext)[which].at[pl.ds(dst_r, len_r), pl.ds(dst_c, len_c)]
        return pltpu.make_async_remote_copy(
            src_ref=dst,
            dst_ref=dst,
            send_sem=kv_send.at[which, n],
            recv_sem=kv_recv.at[which, n],
            device_id=at(0 if step_c else -step_r, -step_c),
            device_id_type=MESH,
        )

    def outgoing(do, ways):
        for n in ways:
            step_r, step_c = AROUND[n]

            @pl.when(exists(step_r, step_c))
            def _():
                do(n)

    def incoming(do, ways):
        for n in ways:
            step_r, step_c = AROUND[n]

            @pl.when(exists(step_r if step_c else -step_r, -step_c))
            def _():
                do(n)

    outgoing(lambda n: kv_copy(0, n).start(), ROWS + COLUMNS)

    def g_copy(k):
        return pltpu.make_async_remote_copy(
            src_ref=g_ref,
            dst_ref=g_all.at[tp],
            send_sem=g_send.at[k - 1],
            recv_sem=g_recv.at[k - 1],
            device_id={"tp": lax.rem(tp + k, tp_n), "ha": ha, "wa": wa},
            device_id_type=MESH,
        )

    for k in range(1, tp_n):
        g_copy(k).start()

    def z_copy(way, step, source):
        where = w_all.at[w_rows(ha * wa_n + source)]
        return pltpu.make_async_remote_copy(
            src_ref=where,
            dst_ref=where,
            send_sem=z_send.at[way, step],
            recv_sem=z_recv.at[way, step],
            device_id={"tp": tp, "ha": ha, "wa": wa + (1, -1)[way]},
            device_id_type=MESH,
        )

    def y_copy(j, source, k, row):
        where = w_all.at[w_rows(row * wa_n + source)]
        return pltpu.make_async_remote_copy(
            src_ref=where,
            dst_ref=where,
            send_sem=y_send.at[j, k - 1],
            recv_sem=y_recv.at[j, k - 1],
            device_id={"tp": tp, "ha": lax.rem(ha + k, ha_n), "wa": wa},
            device_id_type=MESH,
        )

    def next_exists(way):
        return (wa + 1 < wa_n) if way == 0 else (wa >= 1)

    def source_of(way, step):
        source = wa - 1 - step if way == 0 else wa + 1 + step
        return source, ((source >= 0) if way == 0 else (source < wa_n))

    w_own.wait()
    for way in range(2):

        @pl.when(next_exists(way))
        def _():
            z_copy(way, 0, wa).start()

    for k in range(1, ha_n):
        y_copy(0, wa, k, ha).start()
    outgoing(lambda n: kv_copy(1, n).start(), ROWS + COLUMNS)

    def pass_on(step):
        for way in range(2):
            source, there = source_of(way, step)

            @pl.when(there)
            def _():
                z_copy(way, step, source).wait_recv()
                if step + 1 < wa_n - 1:

                    @pl.when(next_exists(way))
                    def _():
                        z_copy(way, step + 1, source).start()

                for k in range(1, ha_n):
                    y_copy(1 + way * (wa_n - 1) + step, source, k, ha).start()

    row_base, col_base = ha * rows, wa * cols
    scale = HEAD**-0.5

    def place(t):
        r, c = t // cols, t % cols
        start_r = jnp.clip(row_base + r - 1, 0, rows * ha_n - 3) - row_base + 1
        start_c = jnp.clip(col_base + c - 1, 0, cols * wa_n - 3) - col_base + 1
        return r, c, start_r, start_c

    def lanes(head):
        return pl.ds(pl.multiple_of(head * HEAD, HEAD), HEAD)

    def window(ext, start_r, start_c, head):
        return ext[pl.ds(start_r, 3), pl.ds(start_c, 3), :, lanes(head)].reshape(9 * tile, HEAD)

    def softmax_heads(first, last):
        @pl.loop(first, last)
        def _(head):
            for t in range(rows * cols):
                r, c, start_r, start_c = place(t)
                query = q_ref[r, c, :, lanes(head)]
                scores = lax.dot_general(
                    window(k_ext, start_r, start_c, head), query, NT, preferred_element_type=f32
                )
                scores = scores * scale
                expo = jnp.exp(scores - jnp.max(scores, axis=0, keepdims=True))
                inverse = 1.0 / jnp.sum(expo, axis=0, keepdims=True)
                probs[head, t] = (expo * inverse).astype(bf16)

    incoming(lambda n: kv_arrival(0, n).wait_recv(), ROWS)
    outgoing(lambda n: kv_copy(0, n).start(), CORNERS)
    k_own.wait()
    incoming(lambda n: kv_arrival(0, n).wait_recv(), COLUMNS + CORNERS)
    chunks = wa_n - 1
    for i in range(chunks):
        softmax_heads(i * heads // chunks, (i + 1) * heads // chunks)
        pass_on(i)
        if i == 0:
            incoming(lambda n: kv_arrival(1, n).wait_recv(), ROWS)
            outgoing(lambda n: kv_copy(1, n).start(), CORNERS)

    g_own.wait()
    for k in range(1, tp_n):
        g_copy(k).wait_recv()
    v_own.wait()
    incoming(lambda n: kv_arrival(1, n).wait_recv(), COLUMNS + CORNERS)
    for k in range(1, ha_n):
        row = lax.rem(ha + ha_n - k, ha_n)
        y_copy(0, wa, k, row).wait_recv()
        for way in range(2):
            for step in range(wa_n - 1):
                source, there = source_of(way, step)

                @pl.when(there)
                def _():
                    y_copy(1 + way * (wa_n - 1) + step, source, k, row).wait_recv()

    block = 256 if feat % 256 == 0 else 128

    @pl.loop(0, feat // block)
    def _(i):
        columns = pl.ds(pl.multiple_of(i * block, block), block)
        for half in range(2):
            m = rows * cols * tile // 2
            total = jnp.zeros((m, block), f32)
            for p in range(tp_n):
                total = total + jnp.dot(
                    g_all[p, half * m : (half + 1) * m, :],
                    w_all[p * feat : (p + 1) * feat, columns],
                    preferred_element_type=f32,
                )
            ga[half * m : (half + 1) * m, columns] = total.astype(bf16)

    def halo_copy(head, n):
        step_r, step_c = AROUND[n]
        src_r, len_r = outer_part(step_r, rows)
        src_c, len_c = outer_part(step_c, cols)
        return pltpu.make_async_remote_copy(
            src_ref=out_halo.at[head, :, pl.ds(src_r, len_r), pl.ds(src_c, len_c)],
            dst_ref=in_halo[n].at[head],
            send_sem=h_send.at[head, n],
            recv_sem=h_recv.at[head, n],
            device_id=at(0 if step_c else step_r, step_c),
            device_id_type=MESH,
        )

    def send_rows(head):
        def add(n):
            step_r, step_c = AROUND[n]
            halo_copy(head, n).wait_recv()
            r, _ = outer_part(step_r, rows)
            c, _ = inner_part(-step_c, cols)
            total = out_halo[head, :, r, c].astype(f32) + in_halo[n][head, :, 0, 0].astype(f32)
            out_halo[head, :, r, c] = total.astype(bf16)

        incoming(add, CORNERS)
        outgoing(lambda n: halo_copy(head, n).start(), ROWS)

    @pl.loop(0, heads)
    def _(head):
        totals[...] = jnp.zeros_like(totals)
        for t in range(rows * cols):
            r, c, start_r, start_c = place(t)
            grad = ga[t * tile : (t + 1) * tile, lanes(head)]
            prob = probs[head, t]
            grad_probs = lax.dot_general(
                window(v_ext, start_r, start_c, head), grad, NT, preferred_element_type=f32
            )
            weighted = prob.astype(f32) * grad_probs
            delta = jnp.sum(weighted, axis=0, keepdims=True)
            grad_scores = ((weighted - prob.astype(f32) * delta) * scale).astype(bf16)
            query = q_ref[r, c, :, lanes(head)]
            keys = window(k_ext, start_r, start_c, head)
            dq_ref[r, c, :, lanes(head)] = lax.dot_general(
                grad_scores, keys, TN, preferred_element_type=f32
            ).astype(bf16)
            shape = (3, 3, tile, HEAD)
            part = (pl.ds(start_r, 3), pl.ds(start_c, 3))
            grad_keys = jnp.dot(grad_scores, query, preferred_element_type=f32)
            totals[0, *part] += grad_keys.reshape(shape)
            grad_values = jnp.dot(prob, grad, preferred_element_type=f32)
            totals[1, *part] += grad_values.reshape(shape)
        own[head] = totals[:, 1 : rows + 1, 1 : cols + 1]
        out_halo[head] = totals[...].astype(bf16)
        outgoing(lambda n: halo_copy(head, n).start(), COLUMNS + CORNERS)

        @pl.when(head > 0)
        def _():
            send_rows(head - 1)

    send_rows(heads - 1)

    @pl.loop(0, heads)
    def _(head):
        for n in COLUMNS + ROWS:
            step_r, step_c = AROUND[n]

            @pl.when(exists(-step_r, -step_c))
            def _():
                halo_copy(head, n).wait_recv()
                to_r, len_r = inner_part(-step_r, rows)
                to_c, len_c = inner_part(-step_c, cols)
                own[head, :, to_r - 1 : to_r - 1 + len_r, to_c - 1 : to_c - 1 + len_c] += in_halo[n][
                    head
                ].astype(f32)

        dk_ref[:, :, :, lanes(head)] = own[head, 0].astype(bf16)
        dv_ref[:, :, :, lanes(head)] = own[head, 1].astype(bf16)

    for which in range(2):
        outgoing(lambda n: kv_copy(which, n).wait_send(), range(8))
    for k in range(1, tp_n):
        g_copy(k).wait_send()
    for way in range(2):

        @pl.when(next_exists(way))
        def _():
            z_copy(way, 0, wa).wait_send()

        for step in range(wa_n - 1):
            source, there = source_of(way, step)

            if step + 1 < wa_n - 1:

                @pl.when(there & next_exists(way))
                def _():
                    z_copy(way, step + 1, source).wait_send()

            @pl.when(there)
            def _():
                for k in range(1, ha_n):
                    y_copy(1 + way * (wa_n - 1) + step, source, k, ha).wait_send()

    for k in range(1, ha_n):
        y_copy(0, wa, k, ha).wait_send()

    @pl.loop(0, heads)
    def _(head):
        outgoing(lambda n: halo_copy(head, n).wait_send(), range(8))


def local(queries, keys, values, grad_out, out_proj):
    frames, rows, cols, tile, feat = queries.shape
    heads = feat // HEAD
    tokens = rows * cols * tile
    tp_n, ha_n, wa_n = sizes = tuple(lax.axis_size(a) for a in ("tp", "ha", "wa"))
    blocks = queries.shape[1:]
    bf16, f32 = jnp.bfloat16, jnp.float32
    vmem, dma = pltpu.VMEM, pltpu.SemaphoreType.DMA
    length = lambda step, count: count if step == 0 else 1
    in_halo = [
        vmem((heads, 2, length(r, rows), length(c, cols), tile, HEAD), bf16) for r, c in AROUND
    ]
    whole = pl.BlockSpec(memory_space=pltpu.VMEM)
    anywhere = pl.BlockSpec(memory_space=pl.ANY)
    hops = wa_n - 1
    outs = pl.pallas_call(
        functools.partial(kernel, sizes),
        out_shape=[jax.ShapeDtypeStruct(blocks, bf16)] * 3,
        in_specs=[whole, anywhere, anywhere, anywhere, anywhere],
        out_specs=[whole] * 3,
        scratch_shapes=[
            vmem((rows + 2, cols + 2, tile, feat), bf16),
            vmem((rows + 2, cols + 2, tile, feat), bf16),
            vmem((tp_n, tokens, feat), bf16),
            vmem((out_proj.shape[0] * ha_n * wa_n, feat), bf16),
            vmem((tokens, feat), bf16),
            vmem((heads, rows * cols, 9 * tile, tile), bf16),
            vmem((2, rows + 2, cols + 2, tile, HEAD), f32),
            vmem((heads, 2, rows, cols, tile, HEAD), f32),
            vmem((heads, 2, rows + 2, cols + 2, tile, HEAD), bf16),
            *in_halo,
            dma((4,)),
            dma((tp_n - 1,)),
            dma((tp_n - 1,)),
            dma((2, 8)),
            dma((2, 8)),
            dma((2, hops)),
            dma((2, hops)),
            dma((1 + 2 * hops, ha_n - 1)),
            dma((1 + 2 * hops, ha_n - 1)),
            dma((heads, 8)),
            dma((heads, 8)),
        ],
        compiler_params=pltpu.CompilerParams(
            collective_id=0, has_side_effects=True, vmem_limit_bytes=60 * 2**20
        ),
    )(
        queries.reshape(blocks),
        keys.reshape(blocks),
        values.reshape(blocks),
        grad_out.reshape(tokens, feat),
        out_proj,
    )
    return tuple(out.reshape(queries.shape) for out in outs)


def solution(mesh):
    tiles = P(None, "ha", "wa", None, "tp")
    return jax.shard_map(
        local,
        mesh=mesh,
        in_specs=(tiles, tiles, tiles, tiles, P(("ha", "wa"), "tp")),
        out_specs=(tiles,) * 3,
        check_vma=False,
    )
```

```python
import functools

import jax
import jax.numpy as jnp
from jax import lax
from jax.experimental import pallas as pl
from jax.experimental.pallas import tpu as pltpu
from jax.sharding import PartitionSpec as P

HEAD = 128
MESH = pl.DeviceIdType.MESH
AROUND = ((0, -1), (0, 1), (-1, 0), (1, 0), (-1, -1), (-1, 1), (1, -1), (1, 1))
COLUMNS, ROWS, CORNERS = (0, 1), (2, 3), (4, 5, 6, 7)
NT = (((1,), (1,)), ((), ()))
TN = (((0,), (0,)), ((), ()))


def inner_part(step, count):
    return {0: (1, count), -1: (1, 1), 1: (count, 1)}[step]


def outer_part(step, count):
    return {0: (1, count), -1: (0, 1), 1: (count + 1, 1)}[step]


def kernel(
    sizes,
    q_ref,
    k_ref,
    v_ref,
    g_ref,
    w_ref,
    dq_ref,
    dk_ref,
    dv_ref,
    k_ext,
    v_ext,
    g_all,
    w_all,
    ga,
    probs,
    totals,
    own,
    out_halo,
    *rest,
):
    in_halo = rest[:8]
    (
        local_sem,
        g_send,
        g_recv,
        kv_send,
        kv_recv,
        z_send,
        z_recv,
        y_send,
        y_recv,
        h_send,
        h_recv,
    ) = rest[8:]
    tp_n, ha_n, wa_n = sizes
    tp, ha, wa = (lax.axis_index(a) for a in ("tp", "ha", "wa"))
    rows, cols, tile, feat = k_ref.shape
    heads = feat // HEAD
    depth = w_ref.shape[0]
    f32, bf16 = jnp.float32, jnp.bfloat16

    def exists(step_r, step_c):
        r, c = ha + step_r, wa + step_c
        return (r >= 0) & (r < ha_n) & (c >= 0) & (c < wa_n)

    def at(step_r, step_c):
        return {"tp": tp, "ha": ha + step_r, "wa": wa + step_c}

    barrier = pltpu.get_barrier_semaphore()
    for k in range(1, tp_n):
        pl.semaphore_signal(
            barrier, inc=1, device_id={"tp": lax.rem(tp + k, tp_n), "ha": ha, "wa": wa}, device_id_type=MESH
        )
    for k in range(1, ha_n):
        pl.semaphore_signal(
            barrier, inc=1, device_id={"tp": tp, "ha": lax.rem(ha + k, ha_n), "wa": wa}, device_id_type=MESH
        )
    greeted = jnp.int32(tp_n - 1 + ha_n - 1)
    for n in COLUMNS:
        step_r, step_c = AROUND[n]
        here = exists(step_r, step_c)
        greeted = greeted + here.astype(jnp.int32)

        @pl.when(here)
        def _():
            pl.semaphore_signal(barrier, inc=1, device_id=at(step_r, step_c), device_id_type=MESH)

    k_own = pltpu.make_async_copy(k_ref, k_ext.at[pl.ds(1, rows), pl.ds(1, cols)], local_sem.at[0])
    v_own = pltpu.make_async_copy(v_ref, v_ext.at[pl.ds(1, rows), pl.ds(1, cols)], local_sem.at[1])
    g_own = pltpu.make_async_copy(g_ref, g_all.at[tp], local_sem.at[2])
    w_rows = lambda block: pl.ds(pl.multiple_of(block * depth, 16), depth)
    w_own = pltpu.make_async_copy(w_ref, w_all.at[w_rows(ha * wa_n + wa)], local_sem.at[3])
    for copy in (k_own, v_own, g_own, w_own):
        copy.start()
    pl.semaphore_wait(barrier, greeted)

    def kv_copy(which, n):
        step_r, step_c = AROUND[n]
        src_c, len_c = inner_part(step_c, cols)
        dst_c, _ = outer_part(-step_c, cols)
        src, dst = ((k_ref, k_ext), (v_ref, v_ext))[which]
        if step_r and step_c:
            src_r, len_r = outer_part(step_r, rows)
            dst_r = src_r
            there = at(0, step_c)
            src = dst.at[pl.ds(src_r, len_r), pl.ds(src_c, len_c)]
        else:
            src_r, len_r = inner_part(step_r, rows)
            dst_r, _ = outer_part(-step_r, rows)
            there = at(step_r, step_c)
            src = src.at[pl.ds(src_r - 1, len_r), pl.ds(src_c - 1, len_c)]
        return pltpu.make_async_remote_copy(
            src_ref=src,
            dst_ref=dst.at[pl.ds(dst_r, len_r), pl.ds(dst_c, len_c)],
            send_sem=kv_send.at[which, n],
            recv_sem=kv_recv.at[which, n],
            device_id=there,
            device_id_type=MESH,
        )

    def kv_arrival(which, n):
        step_r, step_c = AROUND[n]
        dst_r, len_r = outer_part(step_r if step_c else -step_r, rows)
        dst_c, len_c = outer_part(-step_c, cols)
        dst = (k_ext, v_ext)[which].at[pl.ds(dst_r, len_r), pl.ds(dst_c, len_c)]
        return pltpu.make_async_remote_copy(
            src_ref=dst,
            dst_ref=dst,
            send_sem=kv_send.at[which, n],
            recv_sem=kv_recv.at[which, n],
            device_id=at(0 if step_c else -step_r, -step_c),
            device_id_type=MESH,
        )

    def outgoing(do, ways):
        for n in ways:
            step_r, step_c = AROUND[n]

            @pl.when(exists(step_r, step_c))
            def _():
                do(n)

    def incoming(do, ways):
        for n in ways:
            step_r, step_c = AROUND[n]

            @pl.when(exists(step_r if step_c else -step_r, -step_c))
            def _():
                do(n)


    def g_copy(k):
        return pltpu.make_async_remote_copy(
            src_ref=g_ref,
            dst_ref=g_all.at[tp],
            send_sem=g_send.at[k - 1],
            recv_sem=g_recv.at[k - 1],
            device_id={"tp": lax.rem(tp + k, tp_n), "ha": ha, "wa": wa},
            device_id_type=MESH,
        )

    def z_copy(way, step, source):
        where = w_all.at[w_rows(ha * wa_n + source)]
        return pltpu.make_async_remote_copy(
            src_ref=where,
            dst_ref=where,
            send_sem=z_send.at[way, step],
            recv_sem=z_recv.at[way, step],
            device_id={"tp": tp, "ha": ha, "wa": wa + (1, -1)[way]},
            device_id_type=MESH,
        )

    def y_copy(j, source, k, row):
        where = w_all.at[w_rows(row * wa_n + source)]
        return pltpu.make_async_remote_copy(
            src_ref=where,
            dst_ref=where,
            send_sem=y_send.at[j, k - 1],
            recv_sem=y_recv.at[j, k - 1],
            device_id={"tp": tp, "ha": lax.rem(ha + k, ha_n), "wa": wa},
            device_id_type=MESH,
        )

    def next_exists(way):
        return (wa + 1 < wa_n) if way == 0 else (wa >= 1)

    def source_of(way, step):
        source = wa - 1 - step if way == 0 else wa + 1 + step
        return source, ((source >= 0) if way == 0 else (source < wa_n))

    w_own.wait()
    for way in range(2):

        @pl.when(next_exists(way))
        def _():
            z_copy(way, 0, wa).start()

    for k in range(1, ha_n):
        y_copy(0, wa, k, ha).start()
    outgoing(lambda n: kv_copy(0, n).start(), ROWS + COLUMNS)
    for k in range(1, tp_n):
        g_copy(k).start()
    outgoing(lambda n: kv_copy(1, n).start(), ROWS + COLUMNS)

    def pass_on(step):
        for way in range(2):
            source, there = source_of(way, step)

            @pl.when(there)
            def _():
                z_copy(way, step, source).wait_recv()
                if step + 1 < wa_n - 1:

                    @pl.when(next_exists(way))
                    def _():
                        z_copy(way, step + 1, source).start()

                for k in range(1, ha_n):
                    y_copy(1 + way * (wa_n - 1) + step, source, k, ha).start()

    row_base, col_base = ha * rows, wa * cols
    scale = HEAD**-0.5

    def place(t):
        r, c = t // cols, t % cols
        start_r = jnp.clip(row_base + r - 1, 0, rows * ha_n - 3) - row_base + 1
        start_c = jnp.clip(col_base + c - 1, 0, cols * wa_n - 3) - col_base + 1
        return r, c, start_r, start_c

    def lanes(head):
        return pl.ds(pl.multiple_of(head * HEAD, HEAD), HEAD)

    def window(ext, start_r, start_c, head):
        return ext[pl.ds(start_r, 3), pl.ds(start_c, 3), :, lanes(head)].reshape(9 * tile, HEAD)

    def softmax_heads(first, last):
        @pl.loop(first, last)
        def _(head):
            for t in range(rows * cols):
                r, c, start_r, start_c = place(t)
                query = q_ref[r, c, :, lanes(head)]
                scores = lax.dot_general(
                    window(k_ext, start_r, start_c, head), query, NT, preferred_element_type=f32
                )
                scores = scores * scale
                expo = jnp.exp(scores - jnp.max(scores, axis=0, keepdims=True))
                inverse = 1.0 / jnp.sum(expo, axis=0, keepdims=True)
                probs[head, t] = (expo * inverse).astype(bf16)

    pass_on(0)
    incoming(lambda n: kv_arrival(0, n).wait_recv(), ROWS)
    outgoing(lambda n: kv_copy(0, n).start(), CORNERS)
    k_own.wait()
    incoming(lambda n: kv_arrival(0, n).wait_recv(), COLUMNS + CORNERS)
    chunks = wa_n - 1
    for i in range(chunks):
        softmax_heads(i * heads // chunks, (i + 1) * heads // chunks)
        if i + 1 < chunks:
            pass_on(i + 1)
        if i == 0:
            incoming(lambda n: kv_arrival(1, n).wait_recv(), ROWS)
            outgoing(lambda n: kv_copy(1, n).start(), CORNERS)

    g_own.wait()
    for k in range(1, tp_n):
        g_copy(k).wait_recv()
    v_own.wait()
    incoming(lambda n: kv_arrival(1, n).wait_recv(), COLUMNS + CORNERS)
    for k in range(1, ha_n):
        row = lax.rem(ha + ha_n - k, ha_n)
        y_copy(0, wa, k, row).wait_recv()
        for way in range(2):
            for step in range(wa_n - 1):
                source, there = source_of(way, step)

                @pl.when(there)
                def _():
                    y_copy(1 + way * (wa_n - 1) + step, source, k, row).wait_recv()

    block = 256 if feat % 256 == 0 else 128

    @pl.loop(0, feat // block)
    def _(i):
        columns = pl.ds(pl.multiple_of(i * block, block), block)
        for half in range(2):
            m = rows * cols * tile // 2
            total = jnp.zeros((m, block), f32)
            for p in range(tp_n):
                total = total + jnp.dot(
                    g_all[p, half * m : (half + 1) * m, :],
                    w_all[p * feat : (p + 1) * feat, columns],
                    preferred_element_type=f32,
                )
            ga[half * m : (half + 1) * m, columns] = total.astype(bf16)

    def halo_copy(head, n):
        step_r, step_c = AROUND[n]
        src_r, len_r = outer_part(step_r, rows)
        src_c, len_c = outer_part(step_c, cols)
        return pltpu.make_async_remote_copy(
            src_ref=out_halo.at[head, :, pl.ds(src_r, len_r), pl.ds(src_c, len_c)],
            dst_ref=in_halo[n].at[head],
            send_sem=h_send.at[head, n],
            recv_sem=h_recv.at[head, n],
            device_id=at(0 if step_c else step_r, step_c),
            device_id_type=MESH,
        )

    def send_rows(head):
        def add(n):
            step_r, step_c = AROUND[n]
            halo_copy(head, n).wait_recv()
            r, _ = outer_part(step_r, rows)
            c, _ = inner_part(-step_c, cols)
            total = out_halo[head, :, r, c].astype(f32) + in_halo[n][head, :, 0, 0].astype(f32)
            out_halo[head, :, r, c] = total.astype(bf16)

        incoming(add, CORNERS)
        outgoing(lambda n: halo_copy(head, n).start(), ROWS)

    @pl.loop(0, heads)
    def _(head):
        totals[...] = jnp.zeros_like(totals)
        for t in range(rows * cols):
            r, c, start_r, start_c = place(t)
            grad = ga[t * tile : (t + 1) * tile, lanes(head)]
            prob = probs[head, t]
            grad_probs = lax.dot_general(
                window(v_ext, start_r, start_c, head), grad, NT, preferred_element_type=f32
            )
            weighted = prob.astype(f32) * grad_probs
            delta = jnp.sum(weighted, axis=0, keepdims=True)
            grad_scores = ((weighted - prob.astype(f32) * delta) * scale).astype(bf16)
            query = q_ref[r, c, :, lanes(head)]
            keys = window(k_ext, start_r, start_c, head)
            dq_ref[r, c, :, lanes(head)] = lax.dot_general(
                grad_scores, keys, TN, preferred_element_type=f32
            ).astype(bf16)
            shape = (3, 3, tile, HEAD)
            part = (pl.ds(start_r, 3), pl.ds(start_c, 3))
            grad_keys = jnp.dot(grad_scores, query, preferred_element_type=f32)
            totals[0, *part] += grad_keys.reshape(shape)
            grad_values = jnp.dot(prob, grad, preferred_element_type=f32)
            totals[1, *part] += grad_values.reshape(shape)
        own[head] = totals[:, 1 : rows + 1, 1 : cols + 1]
        out_halo[head] = totals[...].astype(bf16)
        outgoing(lambda n: halo_copy(head, n).start(), COLUMNS + CORNERS)

        @pl.when(head > 0)
        def _():
            send_rows(head - 1)

    send_rows(heads - 1)

    @pl.loop(0, heads)
    def _(head):
        for n in COLUMNS + ROWS:
            step_r, step_c = AROUND[n]

            @pl.when(exists(-step_r, -step_c))
            def _():
                halo_copy(head, n).wait_recv()
                to_r, len_r = inner_part(-step_r, rows)
                to_c, len_c = inner_part(-step_c, cols)
                own[head, :, to_r - 1 : to_r - 1 + len_r, to_c - 1 : to_c - 1 + len_c] += in_halo[n][
                    head
                ].astype(f32)

        dk_ref[:, :, :, lanes(head)] = own[head, 0].astype(bf16)
        dv_ref[:, :, :, lanes(head)] = own[head, 1].astype(bf16)

    for which in range(2):
        outgoing(lambda n: kv_copy(which, n).wait_send(), range(8))
    for k in range(1, tp_n):
        g_copy(k).wait_send()
    for way in range(2):

        @pl.when(next_exists(way))
        def _():
            z_copy(way, 0, wa).wait_send()

        for step in range(wa_n - 1):
            source, there = source_of(way, step)

            if step + 1 < wa_n - 1:

                @pl.when(there & next_exists(way))
                def _():
                    z_copy(way, step + 1, source).wait_send()

            @pl.when(there)
            def _():
                for k in range(1, ha_n):
                    y_copy(1 + way * (wa_n - 1) + step, source, k, ha).wait_send()

    for k in range(1, ha_n):
        y_copy(0, wa, k, ha).wait_send()

    @pl.loop(0, heads)
    def _(head):
        outgoing(lambda n: halo_copy(head, n).wait_send(), range(8))


def local(queries, keys, values, grad_out, out_proj):
    frames, rows, cols, tile, feat = queries.shape
    heads = feat // HEAD
    tokens = rows * cols * tile
    tp_n, ha_n, wa_n = sizes = tuple(lax.axis_size(a) for a in ("tp", "ha", "wa"))
    blocks = queries.shape[1:]
    bf16, f32 = jnp.bfloat16, jnp.float32
    vmem, dma = pltpu.VMEM, pltpu.SemaphoreType.DMA
    length = lambda step, count: count if step == 0 else 1
    in_halo = [
        vmem((heads, 2, length(r, rows), length(c, cols), tile, HEAD), bf16) for r, c in AROUND
    ]
    whole = pl.BlockSpec(memory_space=pltpu.VMEM)
    anywhere = pl.BlockSpec(memory_space=pl.ANY)
    hops = wa_n - 1
    outs = pl.pallas_call(
        functools.partial(kernel, sizes),
        out_shape=[jax.ShapeDtypeStruct(blocks, bf16)] * 3,
        in_specs=[whole, anywhere, anywhere, anywhere, anywhere],
        out_specs=[whole] * 3,
        scratch_shapes=[
            vmem((rows + 2, cols + 2, tile, feat), bf16),
            vmem((rows + 2, cols + 2, tile, feat), bf16),
            vmem((tp_n, tokens, feat), bf16),
            vmem((out_proj.shape[0] * ha_n * wa_n, feat), bf16),
            vmem((tokens, feat), bf16),
            vmem((heads, rows * cols, 9 * tile, tile), bf16),
            vmem((2, rows + 2, cols + 2, tile, HEAD), f32),
            vmem((heads, 2, rows, cols, tile, HEAD), f32),
            vmem((heads, 2, rows + 2, cols + 2, tile, HEAD), bf16),
            *in_halo,
            dma((4,)),
            dma((tp_n - 1,)),
            dma((tp_n - 1,)),
            dma((2, 8)),
            dma((2, 8)),
            dma((2, hops)),
            dma((2, hops)),
            dma((1 + 2 * hops, ha_n - 1)),
            dma((1 + 2 * hops, ha_n - 1)),
            dma((heads, 8)),
            dma((heads, 8)),
        ],
        compiler_params=pltpu.CompilerParams(
            collective_id=0, has_side_effects=True, vmem_limit_bytes=60 * 2**20
        ),
    )(
        queries.reshape(blocks),
        keys.reshape(blocks),
        values.reshape(blocks),
        grad_out.reshape(tokens, feat),
        out_proj,
    )
    return tuple(out.reshape(queries.shape) for out in outs)


def solution(mesh):
    tiles = P(None, "ha", "wa", None, "tp")
    return jax.shard_map(
        local,
        mesh=mesh,
        in_specs=(tiles, tiles, tiles, tiles, P(("ha", "wa"), "tp")),
        out_specs=(tiles,) * 3,
        check_vma=False,
    )
```
